256 devices in a mesh: wide: 32 (over y_hi, z, core), narrow: 8 (over x, y_lo).
Axes of the slice: x: 4, y: 4 (y_hi: 2, y_lo: 2; y = y_hi * 2 + y_lo), z: 8, core: 2. Of those that a mesh axis runs over, the one named last changes fastest.
Arguments:
- gradient: bfloat16 [16384, 53248], P('wide', 'narrow'), may hold values from -6 to 6
- right_panel: float32 [53248, 512], P('narrow', 'wide'), may hold values from -0.046875 to 0.046875
- left_panel: bfloat16 [16384, 1024], P('wide'), may hold values from -0.09375 to 0.09375
- second_moment: float32 [1024, 512], P('wide', 'narrow'), may hold values from 0.1 to 10
Outputs:
- moment_new: float32 [1024, 512], P('wide', 'narrow')
- step_update: float32 [1024, 512], P('wide', 'narrow')
The draws below stay inside these ranges and needn't reach their ends.
All inputs are finite; a program needn't handle non-finite values.
Results may differ from the reference program's by a relative error of at most 0.0003.
Values sent between devices are 32-bit elements; how exact they have to be, the bound alone decides.
A program may use at most 64 MiB of HBM per device.

```python
import math
import jax
import jax.numpy as jnp
from jax import lax

D = 16384
FF = 53248
PANEL = 512
LEFT = 1024


def spiked(drawn, key, source, target, shards_of, factor):
    owner, partner = [(jnp.arange(drawn.shape[position]) // (drawn.shape[position] // shards_of)).reshape([-1 if axis == position else 1 for axis in range(drawn.ndim)]) for position in (source, target)]
    chosen = jax.random.permutation(key, shards_of)[partner]
    strong = (owner == chosen) | (owner == (partner + shards_of // 2) % shards_of)
    return jnp.where(strong, factor * drawn, drawn)


def block_levels(key, extent, shards, smallest, high):
    factor_of, own = 1.0, jax.random.fold_in(key, 6)
    for dim, shards_of in shards:
        steps = jnp.exp(jax.random.uniform(jax.random.fold_in(own, dim), (shards_of,), jnp.float32, smallest / len(shards), high / len(shards)))
        factor_of = factor_of * jnp.repeat(steps, extent[dim] // shards_of).reshape([-1 if axis == dim else 1 for axis in range(len(extent))])
    return factor_of


def noise(rng, extent, width, bound, cuts=(), held_as=jnp.bfloat16):
    values = jax.random.normal(rng, extent, jnp.float32) * width
    if len(cuts) > 0:
        values = block_levels(rng, extent, cuts, -0.22, 0.18) * values
    return jnp.clip(values, min=-bound, max=bound).astype(held_as)


def bell_draw_with(key, shape, deviation, reach, shards, heavy, dtype=jnp.bfloat16):
    result = deviation * jax.random.normal(key, shape, jnp.float32)
    if shards:
        result = result * block_levels(key, shape, shards, -0.22, 0.18)
    return jnp.clip(spiked(result, jax.random.fold_in(key, 3), *heavy), -reach, reach).astype(dtype)


def setup_inputs(seed: int = 0) -> dict:
    key_of = jax.random.split(jax.random.key(seed), 5)
    return {
        "gradient": noise(key_of[0], (D, FF), 1.0, 6.0, ((0, 32), (1, 8))),
        "right_panel": bell_draw_with(key_of[1], (FF, PANEL), FF ** -0.5, 0.046875, ((0, 8), (1, 32)), (0, 1, 32, 2.75), jnp.float32),
        "left_panel": bell_draw_with(key_of[2], (D, LEFT), D ** -0.5, 0.09375, ((0, 32),), (0, 1, 32, 2.75)),
        "second_moment": jnp.clip(jnp.exp(math.log(10.0) - 4.6051702 * jax.random.uniform(key_of[3], (LEFT, PANEL), jnp.float32) ** block_levels(key_of[3], (LEFT, PANEL), ((0, 32), (1, 8)), -0.2, 0.2)), 0.1, 10.0),
    }


def reference(gradient, right_panel, left_panel, second_moment):
    unit = math.gcd(D, 512)
    blocks = gradient.reshape(D // unit, unit, FF)

    def project(block):
        return jnp.dot(block.astype(jnp.float32), right_panel, precision=lax.Precision.HIGHEST, preferred_element_type=jnp.float32)
    hidden_panel = lax.map(project, blocks).reshape(D, PANEL)
    rotated = lax.dot_general(left_panel.astype(jnp.float32), hidden_panel, (((0,), (0,)), ((), ())), precision=lax.Precision.HIGHEST, preferred_element_type=jnp.float32)
    moment_new = 0.95 * second_moment + 0.05 * rotated * rotated
    step_update = rotated / (jnp.sqrt(moment_new) + 1e-08)
    return (moment_new, step_update)
```

```python
import functools

import jax
import jax.numpy as jnp
from jax import lax
from jax.experimental import pallas as pl
from jax.experimental.pallas import tpu as pltpu
from jax.sharding import PartitionSpec as P

MESH = pl.DeviceIdType.MESH
NT = (((1,), (1,)), ((), ()))
F32, BF16 = jnp.float32, jnp.bfloat16

FFL = 6656
ROWS = 512
LEFT = 1024
TILE = 128
SPLIT = 26 * TILE
A, B, A2 = 0, 1, 2
HALF_A = 14 * TILE
HALF_B = 12 * TILE


def lanes(s, way, kind):
    if kind == B:
        if s < 4:
            return SPLIT, FFL - SPLIT
        return (SPLIT, HALF_B) if way == 0 else (SPLIT + HALF_B, FFL - SPLIT - HALF_B)
    if s < 4:
        return 0, SPLIT
    return (0, HALF_A) if way == 0 else (HALF_A, SPLIT - HALF_A)


def unit(s, way, other):
    if s == 0:
        return other
    if s == 4:
        return 14 + other
    return 2 + (s - 1) * 4 + way * 2 + other


def kernel(
    rt_ref, g_ref, l_ref, sm_ref, mom_ref, step_ref,
    panel, grad, left, left_t, acc, hidden, parts, stack, rot, gathered,
    own_sem, g_sem, l_sem, z_send, z_recv, y_send, y_recv, s_send, s_recv,
    n_send, n_recv, w_send, w_recv,
):
    w, n = lax.axis_index("wide"), lax.axis_index("narrow")
    yh, z, core = w // 16, lax.rem(w // 2, 8), lax.rem(w, 2)

    def at(y_hi, zz, cc):
        return (y_hi * 16 + lax.rem(zz + 16, 8) * 2 + cc, n)

    ring = (at(yh, z + 1, core), at(yh, z - 1, core))
    across = at(1 - yh, z, core)
    sibling = at(yh, z, 1 - core)

    own = pltpu.make_async_copy(rt_ref, panel.at[pl.ds(core * 2, 2)], own_sem)
    own.start()
    load_g = pltpu.make_async_copy(g_ref, grad, g_sem)
    load_g.start()
    load_l = pltpu.make_async_copy(l_ref, left, l_sem)
    load_l.start()

    barrier = pltpu.get_barrier_semaphore()
    greet = [*ring, at(yh, z + 2, core), at(yh, z - 2, core), across, sibling]
    greet += [(w, lax.rem(n + i, 8)) for i in range(1, 8)]
    for device in greet:
        pl.semaphore_signal(barrier, inc=1, device_id=device, device_id_type=MESH)
    own.wait()
    pl.semaphore_wait(barrier, len(greet))

    def block(u, first, size):
        return panel.at[pl.ds(u * 4 + core * 2, 2), :, pl.ds(first, size)]

    def remote(src, dst, send, recv, device):
        return pltpu.make_async_remote_copy(
            src_ref=src, dst_ref=dst, send_sem=send, recv_sem=recv, device_id=device, device_id_type=MESH
        )

    started = []

    def start(copy):
        copy.start()
        started.append(copy)

    def along_z(s, way, kind):
        first, size = lanes(s, way, kind)
        other = int(kind == A2)
        which = way * 12 + (s - 1) * 3 + kind
        return remote(
            block(unit(s - 1, way, other), first, size),
            block(unit(s, way, other), first, size),
            z_send.at[which], z_recv.at[which], ring[way],
        )

    def along_y(s, way, kind):
        first, size = lanes(s, way, kind)
        which = int(kind == B) if s == 0 else 2 + (s - 1) * 2 + way
        return remote(
            block(unit(s, way, 0), first, size), block(unit(s, way, 1), first, size),
            y_send.at[which], y_recv.at[which], across,
        )

    def to_sibling(u, group, first=0, size=FFL, slot=0):
        part = block(u, first, size)
        start(remote(part, part, s_send.at[u + 2 * slot], s_recv.at[group], sibling))

    def wait_bytes(ref, sem):
        pltpu.make_async_copy(ref, ref, sem).wait()

    def multiply(first_block, blocks, first, size, step, fresh):
        rows = blocks * 8

        def body(i, carry):
            cols = pl.ds(pl.multiple_of(first + i * step, TILE), step)
            value = panel[pl.ds(first_block, blocks), :, cols].reshape(rows, step)
            high = value.astype(BF16)
            low = (value - high.astype(F32)).astype(BF16)
            both = jnp.concatenate([high, low], axis=0)
            acc[: 2 * rows] += lax.dot_general(both, grad[:, cols], NT, preferred_element_type=F32)
            return carry

        if fresh:
            acc[: 2 * rows] = jnp.zeros((2 * rows, ROWS), F32)
        lax.fori_loop(0, size // step, body, 0)

    def scatter(s, first_unit, units):
        rows = units * 32
        hidden[first_unit * 32 : first_unit * 32 + rows] = acc[:rows] + acc[rows : 2 * rows]
        for k in range(units):
            u, way, other = first_unit + k, (k // 2 if 0 < s < 4 else 0), k % 2
            zz = lax.rem(z + (s if way == 1 else -s) + 8, 8)
            keeper = (yh if other == 0 else 1 - yh) * 4 + zz // 2
            ahead = lax.rem(keeper - n + 8, 8)
            place = pl.ds(pl.multiple_of(lax.rem(zz, 2) * 32, 32), 32)

            @pl.when(ahead == 0)
            def _():
                parts[7, place, :] = hidden[u * 32 : u * 32 + 32]

            @pl.when(ahead != 0)
            def _():
                remote(
                    hidden.at[pl.ds(u * 32, 32)], parts.at[7 - ahead, place], n_send, n_recv, (w, keeper)
                ).start()

    def rotate():
        wait_bytes(parts.at[pl.ds(0, 7)], n_recv)
        total = parts[0]
        for i in range(1, 8):
            total = total + parts[i]
        high = total.astype(BF16)
        stack[:64] = high
        stack[64:] = (total - high.astype(F32)).astype(BF16)

        def body(i, carry):
            out = lax.dot_general(
                left_t[pl.ds(pl.multiple_of(i * 256, 256), 256), :], stack[...], NT, preferred_element_type=F32
            )
            out = out + pltpu.roll(out, 64, 1)
            out = out.reshape(8, 2, 16, 128)
            lane = lax.broadcasted_iota(jnp.int32, (8, 16, 128), 2)
            rot[pl.ds(i * 8, 8)] = jnp.where(lane < 64, out[:, 0], out[:, 1])
            return carry

        lax.fori_loop(0, 4, body, 0)

        def send(i, carry):
            target = lax.rem(w + i, 32)
            remote(rot.at[target], gathered.at[i - 1], w_send, w_recv, (target, n)).start()
            return carry

        lax.fori_loop(1, 32, send, 0)
        gathered[31] = rot[w]

    first_z = 2 * lax.rem(n, 4)

    def distance(a):
        there = lax.rem(z - a + 8, 8)
        return jnp.minimum(there, lax.rem(8 - there, 8))

    last_step = jnp.maximum(distance(first_z), distance(first_z + 1))

    start(along_y(0, 0, A))
    for way in (0, 1):
        start(along_z(1, way, B))
    to_sibling(0, 0)
    for way in (0, 1):
        start(along_z(1, way, A))
    start(along_y(0, 0, B))

    load_l.wait()

    def turn(i, carry):
        cols = pl.ds(pl.multiple_of(i * 256, 256), 256)
        left_t[cols, :] = left[:, cols].T
        return carry

    lax.fori_loop(0, 4, turn, 0)

    along_y(0, 0, A).wait_recv()
    for way in (0, 1):
        start(along_z(1, way, A2))

    def forward_b(s):
        for way in (0, 1):
            along_z(s, way, B).wait_recv()
            if s < 4:
                start(along_z(s + 1, way, B))
            start(along_y(s, way, B))

    def forward_a(s):
        for way in (0, 1):
            along_z(s, way, A).wait_recv()
            if s < 4:
                start(along_z(s + 1, way, A))
                to_sibling(unit(s, way, 0), s)

    def forward_a2(s):
        for way in (0, 1):
            along_z(s, way, A2).wait_recv()
            if s < 4:
                start(along_z(s + 1, way, A2))

    def settle_y(s):
        for way in (0, 1):
            along_y(s, way, B).wait_recv()
            if s < 4:
                to_sibling(unit(s, way, 1), s)

    def compute(s):
        wait_bytes(panel.at[pl.ds(0, 8)], s_recv.at[s])
        multiply(unit(s, 0, 0) * 4, 16, 0, FFL, 512, True)
        scatter(s, unit(s, 0, 0), 4)

    forward_b(1)
    along_y(0, 0, B).wait_recv()
    to_sibling(1, 0)
    forward_a(1)
    load_g.wait()
    wait_bytes(panel.at[pl.ds(0, 4)], s_recv.at[0])
    multiply(0, 8, 0, FFL, 512, True)
    scatter(0, 0, 2)
    forward_a2(1)
    settle_y(1)
    forward_b(2)
    compute(1)
    forward_a(2)
    forward_a2(2)
    settle_y(2)
    forward_b(3)
    compute(2)
    forward_a(3)

    @pl.when(last_step <= 2)
    def _():
        rotate()

    forward_a2(3)
    settle_y(3)
    forward_b(4)
    to_sibling(14, 4, SPLIT, FFL - SPLIT, 0)
    compute(3)
    forward_a(4)
    to_sibling(14, 5, 0, SPLIT, 1)
    settle_y(4)
    to_sibling(15, 4, SPLIT, FFL - SPLIT, 0)
    forward_a2(4)
    to_sibling(15, 5, 0, SPLIT, 1)
    wait_bytes(panel.at[pl.ds(0, 4), :, pl.ds(SPLIT, FFL - SPLIT)], s_recv.at[4])
    multiply(56, 8, SPLIT, FFL - SPLIT, 256, True)
    wait_bytes(panel.at[pl.ds(0, 4), :, pl.ds(0, SPLIT)], s_recv.at[5])
    multiply(56, 8, 0, SPLIT, 256, False)
    scatter(4, 14, 2)

    @pl.when(last_step > 2)
    def _():
        rotate()

    wait_bytes(gathered.at[pl.ds(0, 31)], w_recv)
    rotated = jnp.sum(gathered[...], axis=0)
    rotated = jnp.concatenate([rotated, pltpu.roll(rotated, 64, 1)], axis=0)[:, :64]
    moment = 0.95 * sm_ref[...] + 0.05 * rotated * rotated
    mom_ref[...] = moment
    step_ref[...] = rotated / (jnp.sqrt(moment) + 1e-08)

    for copy in started:
        copy.wait_send()
    wait_bytes(hidden.at[pl.ds(0, 448)], n_send)
    wait_bytes(gathered.at[pl.ds(0, 31)], w_send)


def shards(gradient, right_panel, left_panel, second_moment):
    panel_t = right_panel.T.reshape(2, 8, FFL)
    anywhere = pl.BlockSpec(memory_space=pl.ANY)
    vmem = pl.BlockSpec(memory_space=pltpu.VMEM)
    dma = pltpu.SemaphoreType.DMA
    return pl.pallas_call(
        kernel,
        out_shape=[jax.ShapeDtypeStruct(second_moment.shape, F32)] * 2,
        in_specs=[anywhere, anywhere, anywhere, vmem],
        out_specs=[vmem, vmem],
        scratch_shapes=[
            pltpu.VMEM((64, 8, FFL), F32),
            pltpu.VMEM((ROWS, FFL), BF16),
            pltpu.VMEM((ROWS, LEFT), BF16),
            pltpu.VMEM((LEFT, ROWS), BF16),
            pltpu.VMEM((256, ROWS), F32),
            pltpu.VMEM((512, ROWS), F32),
            pltpu.VMEM((8, 64, ROWS), F32),
            pltpu.VMEM((128, ROWS), BF16),
            pltpu.VMEM((32, 16, 128), F32),
            pltpu.VMEM((32, 16, 128), F32),
            dma, dma, dma, dma((24,)), dma((24,)), dma((10,)), dma((10,)), dma((18,)), dma((6,)),
            dma, dma, dma, dma,
        ],
        compiler_params=pltpu.CompilerParams(
            collective_id=0, has_side_effects=True, vmem_limit_bytes=60 * 2**20
        ),
    )(panel_t, gradient, left_panel, second_moment)


def solution(mesh):
    placed = (P("wide", "narrow"), P("narrow", "wide"), P("wide", None), P("wide", "narrow"))
    return jax.shard_map(
        shards,
        mesh=mesh,
        in_specs=placed,
        out_specs=(P("wide", "narrow"), P("wide", "narrow")),
        check_vma=False,
    )
```

```python
import functools

import jax
import jax.numpy as jnp
from jax import lax
from jax.experimental import pallas as pl
from jax.experimental.pallas import tpu as pltpu
from jax.sharding import PartitionSpec as P

MESH = pl.DeviceIdType.MESH
NT = (((1,), (1,)), ((), ()))
F32, BF16 = jnp.float32, jnp.bfloat16

FFL = 6656
ROWS = 512
LEFT = 1024
TILE = 128
SPLIT = 24 * TILE
DIRECT = 3
A, B, A2 = 0, 1, 2
HALF_A = 12 * TILE
HALF_B = 14 * TILE


def lanes(s, way, kind):
    if kind == B:
        if s < 4:
            return SPLIT, FFL - SPLIT
        return (SPLIT, HALF_B) if way == 0 else (SPLIT + HALF_B, FFL - SPLIT - HALF_B)
    if s < 4:
        return 0, SPLIT
    return (0, HALF_A) if way == 0 else (HALF_A, SPLIT - HALF_A)


def unit(s, way, other):
    if s == 0:
        return other
    if s == 4:
        return 14 + other
    return 2 + (s - 1) * 4 + other * 2 + way


def kernel(
    rt_ref, g_ref, l_ref, sm_ref, mom_ref, step_ref,
    panel, grad, left, left_t, acc, hidden, parts, x_parts, y_out, y_in, mine, stack,
    rot, rot_in, gathered, last, last_in, last_gathered,
    own_sem, g_sem, l_sem, z_send, z_recv, y_send, y_recv, s_send, s_recv,
    n_send, n_recv, p_send, p_recv, x_recv, w_send, w_recv,
    e_send, e_recv, q_send, q_recv,
):
    w, n = lax.axis_index("wide"), lax.axis_index("narrow")
    yh, z, core = w // 16, lax.rem(w // 2, 8), lax.rem(w, 2)

    def at(y_hi, zz, cc):
        return (y_hi * 16 + lax.rem(zz + 16, 8) * 2 + cc, n)

    ring = (at(yh, z + 1, core), at(yh, z - 1, core))
    across = at(1 - yh, z, core)
    sibling = at(yh, z, 1 - core)

    own = pltpu.make_async_copy(rt_ref, panel.at[pl.ds(core * 2, 2)], own_sem)
    own.start()
    load_g = pltpu.make_async_copy(g_ref, grad, g_sem)
    load_g.start()
    load_l = pltpu.make_async_copy(l_ref, left, l_sem)
    load_l.start()

    barrier = pltpu.get_barrier_semaphore()
    greet = [*ring, across, sibling]
    greet += [(w, lax.rem(n + i, 8)) for i in range(1, 8)]
    for device in greet:
        pl.semaphore_signal(barrier, inc=1, device_id=device, device_id_type=MESH)
    own.wait()
    pl.semaphore_wait(barrier, len(greet))

    def block(u, first, size):
        return panel.at[pl.ds(u * 4 + core * 2, 2), :, pl.ds(first, size)]

    def remote(src, dst, send, recv, device):
        return pltpu.make_async_remote_copy(
            src_ref=src, dst_ref=dst, send_sem=send, recv_sem=recv, device_id=device, device_id_type=MESH
        )

    started = []

    def start(copy):
        copy.start()
        started.append(copy)

    def along_z(s, way, kind):
        first, size = lanes(s, way, kind)
        other = int(kind == A2)
        which = way * 12 + (s - 1) * 3 + kind
        return remote(
            block(unit(s - 1, way, other), first, size),
            block(unit(s, way, other), first, size),
            z_send.at[which], z_recv.at[which], ring[way],
        )

    def along_y(s, way, kind):
        first, size = lanes(s, way, kind)
        which = int(kind == B) if s == 0 else 2 + (s - 1) * 2 + way
        return remote(
            block(unit(s, way, 0), first, size), block(unit(s, way, 1), first, size),
            y_send.at[which], y_recv.at[which], across,
        )

    def to_sibling(u, group, first=0, size=FFL, slot=0):
        part = block(u, first, size)
        start(remote(part, part, s_send.at[u + 2 * slot], s_recv.at[group], sibling))

    def wait_bytes(ref, sem):
        pltpu.make_async_copy(ref, ref, sem).wait()

    def multiply(first_block, blocks, first, size, step, fresh):
        rows = blocks * 8

        def body(i, carry):
            cols = pl.ds(pl.multiple_of(first + i * step, TILE), step)
            value = panel[pl.ds(first_block, blocks), :, cols].reshape(rows, step)
            high = value.astype(BF16)
            low = (value - high.astype(F32)).astype(BF16)
            both = jnp.concatenate([high, low], axis=0)
            acc[: 2 * rows] += lax.dot_general(both, grad[:, cols], NT, preferred_element_type=F32)
            return carry

        if fresh:
            acc[: 2 * rows] = jnp.zeros((2 * rows, ROWS), F32)
        lax.fori_loop(0, size // step, body, 0)

    def hidden_copy(s, u):
        way, other = (u % 2, (u - 2) % 4 // 2) if 0 < s < 4 else (0, u % 2)
        zz = lax.rem(z + (s if way == 1 else -s) + 8, 8)
        there = yh if other == 0 else 1 - yh
        source = hidden.at[pl.ds(u * 32, 32)]
        if s >= DIRECT:
            keeper = there * 4 + zz // 2
            ahead = lax.rem(keeper - n + 8, 8)
            half = lax.rem(zz, 2)
            return (
                remote(source, parts.at[7 - ahead, half], n_send.at[u], n_recv.at[half], (w, keeper)),
                source, parts.at[7, half], ahead,
            )
        keeper = there * 2 + zz // 4
        ahead = lax.rem(keeper - n // 2 + 4, 4)
        quarter = lax.rem(zz, 4)
        device = (w, keeper * 2 + lax.rem(n, 2))
        return (
            remote(source, x_parts.at[3 - ahead, quarter], n_send.at[u], x_recv.at[quarter], device),
            source, x_parts.at[3, quarter], ahead,
        )

    scattered = []

    def scatter(s, first_unit, units):
        rows = units * 32
        hidden[first_unit * 32 : first_unit * 32 + rows] = acc[:rows] + acc[rows : 2 * rows]
        for u in range(first_unit, first_unit + units):
            copy, source, here, ahead = hidden_copy(s, u)
            scattered.append((s, u))

            @pl.when(ahead == 0)
            def _():
                here[...] = source[...]

            @pl.when(ahead != 0)
            def _():
                copy.start()

    def distance(a):
        there = lax.rem(z - a + 8, 8)
        return jnp.minimum(there, lax.rem(8 - there, 8))

    x_first = 4 * lax.rem(n // 2, 2)
    y_lo = lax.rem(n, 2)

    def to_pair(q):
        return remote(y_out.at[q % 2], y_in.at[q % 2], p_send.at[q % 2], p_recv.at[q % 2], (w, n + 1 - 2 * y_lo))

    def reduce_x(s):
        for q in range(4):

            @pl.when(distance(x_first + q) == s)
            def _():
                wait_bytes(x_parts.at[pl.ds(0, 3), q], x_recv.at[q])
                total = x_parts[0, q] + x_parts[1, q] + x_parts[2, q] + x_parts[3, q]

                @pl.when(y_lo == q // 2)
                def _():
                    mine[q % 2] = total

                @pl.when(y_lo != q // 2)
                def _():
                    y_out[q % 2] = total
                    to_pair(q).start()

    first_z = 2 * lax.rem(n, 4)

    spot = w // 2

    def fill_stack(total):
        high = total.astype(BF16)
        stack[:64] = high
        stack[64:] = (total - high.astype(F32)).astype(BF16)

    def rotated_rows(i):
        cols = pl.ds(pl.multiple_of(i * 256, 256), 256)
        out = lax.dot_general(left_t[cols, :], stack[...], NT, preferred_element_type=F32)
        return out + pltpu.roll(out, 64, 1)

    swap_rot = remote(rot.at[1 - core], rot_in, e_send.at[0], e_recv.at[0], sibling)
    swap_last = remote(last.at[1 - core], last_in, e_send.at[1], e_recv.at[1], sibling)

    def rotate_start():
        for half in (0, 1):
            d = distance(first_z + half)

            @pl.when(d == 4)
            def _():
                mine[half] = jnp.zeros((32, ROWS), F32)

            @pl.when(d == DIRECT)
            def _():
                wait_bytes(parts.at[pl.ds(0, 7), half], n_recv.at[half])
                total = parts[0, half]
                for i in range(1, 8):
                    total = total + parts[i, half]
                mine[half] = total

            @pl.when(d < DIRECT)
            def _():
                wait_bytes(y_in.at[half], p_recv.at[half])
                mine[half] += y_in[half]

        fill_stack(mine[...].reshape(64, ROWS))

        def body(i, carry):
            out = rotated_rows(i).reshape(4, 2, 2, 16, 128)
            lane = lax.broadcasted_iota(jnp.int32, (4, 16, 128), 2)
            for c in (0, 1):
                rot[c, pl.ds(i * 4, 4)] = jnp.where(lane < 64, out[:, c, 0], out[:, c, 1])
            return carry

        lax.fori_loop(0, 4, body, 0)
        swap_rot.start()

    def rotate_finish():
        swap_rot.wait_recv()

        def add(k, carry):
            rot[core, k] += rot_in[k]
            return carry

        lax.fori_loop(0, 16, add, 0)

        def send(i, carry):
            k = lax.rem(spot + i, 16)
            remote(rot.at[core, k], gathered.at[i - 1], w_send, w_recv, (k * 2 + core, n)).start()
            return carry

        lax.fori_loop(1, 16, send, 0)
        gathered[15] = rot[core, spot]

    def last_start():
        fill_stack(acc[:64] + acc[64:128])

        def body(i, carry):
            out = rotated_rows(i)
            turned = pltpu.roll(out, 32, 1).reshape(4, 2, 4, 8, 128)
            out = out.reshape(4, 2, 4, 8, 128)
            which = lax.broadcasted_iota(jnp.int32, (4, 8, 128), 2) // 32
            for c in (0, 1):
                for other in (0, 1):
                    even, odd = (out, turned) if other == 0 else (turned, out)
                    value = jnp.where(which == 0, even[:, c, 0], odd[:, c, 1])
                    value = jnp.where(which == 2, even[:, c, 2], value)
                    last[c, pl.ds(i * 4, 4), other] = jnp.where(which == 3, odd[:, c, 3], value)
            return carry

        lax.fori_loop(0, 4, body, 0)
        swap_last.start()

    far_chip = lax.rem(z + 4, 8)
    own_last = lax.rem(n, 4) == far_chip // 2

    def last_finish():
        swap_last.wait_recv()

        def add(k, carry):
            last[core, k] += last_in[k]
            return carry

        lax.fori_loop(0, 16, add, 0)
        half = lax.rem(z, 2)
        slot = half * 16 + yh * 8 + n

        def send(i, carry):
            k = lax.rem(spot + i, 16)
            for other in (0, 1):
                keeper = (yh if other == 0 else 1 - yh) * 4 + far_chip // 2
                here = (k == spot) & (keeper == n)
                source, target = last.at[core, k, other], last_gathered.at[slot]

                @pl.when(here)
                def _():
                    pltpu.make_async_copy(source, target, q_recv.at[half]).start()

                @pl.when(jnp.logical_not(here))
                def _():
                    remote(source, target, q_send, q_recv.at[half], (k * 2 + core, keeper)).start()

            return carry

        lax.fori_loop(0, 16, send, 0)

    last_step = jnp.maximum(distance(first_z), distance(first_z + 1))

    start(along_y(0, 0, A))
    for way in (0, 1):
        start(along_z(1, way, B))
    to_sibling(0, 0)
    for way in (0, 1):
        start(along_z(1, way, A))
    start(along_y(0, 0, B))

    load_l.wait()

    def turn(i, carry):
        cols = pl.ds(pl.multiple_of(i * 256, 256), 256)
        left_t[cols, :] = left[:, cols].T
        return carry

    lax.fori_loop(0, 4, turn, 0)

    along_y(0, 0, A).wait_recv()
    for way in (0, 1):
        start(along_z(1, way, A2))

    def forward_b(s):
        for way in (0, 1):
            along_z(s, way, B).wait_recv()
            if s < 4:
                start(along_z(s + 1, way, B))
            start(along_y(s, way, B))

    def forward_a(s):
        for way in (0, 1):
            along_z(s, way, A).wait_recv()
            if s < 4:
                start(along_z(s + 1, way, A))
                to_sibling(unit(s, way, 0), s)

    def forward_a2(s):
        for way in (0, 1):
            along_z(s, way, A2).wait_recv()
            if s < 4:
                start(along_z(s + 1, way, A2))

    def settle_y(s):
        for way in (0, 1):
            along_y(s, way, B).wait_recv()
            if s < 4:
                to_sibling(unit(s, way, 1), 6 if s == 3 else s)

    def compute(s):
        wait_bytes(panel.at[pl.ds(0, 8)], s_recv.at[s])
        multiply(unit(s, 0, 0) * 4, 16, 0, FFL, 1664, True)
        scatter(s, unit(s, 0, 0), 4)

    forward_b(1)
    forward_a(1)
    along_y(0, 0, B).wait_recv()
    to_sibling(1, 0)
    load_g.wait()
    wait_bytes(panel.at[pl.ds(0, 4)], s_recv.at[0])
    multiply(0, 8, 0, FFL, 1664, True)
    scatter(0, 0, 2)
    forward_b(2)
    forward_a2(1)
    settle_y(1)
    forward_a(2)
    compute(1)
    reduce_x(0)
    forward_b(3)
    forward_a2(2)
    settle_y(2)
    compute(2)
    reduce_x(1)
    forward_a(3)
    forward_b(4)
    to_sibling(14, 4, SPLIT, FFL - SPLIT, 0)
    wait_bytes(panel.at[pl.ds(0, 4)], s_recv.at[3])
    multiply(unit(3, 0, 0) * 4, 8, 0, FFL, 1664, True)
    scatter(3, unit(3, 0, 0), 2)
    reduce_x(2)
    forward_a2(3)
    settle_y(3)
    wait_bytes(panel.at[pl.ds(0, 4)], s_recv.at[6])
    multiply(unit(3, 0, 1) * 4, 8, 0, FFL, 1664, True)
    scatter(3, unit(3, 0, 1), 2)
    forward_a(4)
    to_sibling(14, 5, 0, SPLIT, 1)

    @pl.when(last_step <= 2)
    def _():
        rotate_start()

    forward_a2(4)
    to_sibling(15, 5, 0, SPLIT, 1)
    settle_y(4)
    to_sibling(15, 4, SPLIT, FFL - SPLIT, 0)
    wait_bytes(panel.at[pl.ds(0, 4), :, pl.ds(0, SPLIT)], s_recv.at[5])
    multiply(56, 8, 0, SPLIT, SPLIT // 2, True)
    wait_bytes(panel.at[pl.ds(0, 4), :, pl.ds(SPLIT, FFL - SPLIT)], s_recv.at[4])
    multiply(56, 8, SPLIT, FFL - SPLIT, (FFL - SPLIT) // 2, False)
    last_start()

    @pl.when(last_step <= 2)
    def _():
        rotate_finish()

    @pl.when(last_step > 2)
    def _():
        rotate_start()

    last_finish()

    @pl.when(last_step > 2)
    def _():
        rotate_finish()

    wait_bytes(gathered.at[pl.ds(0, 15)], w_recv)
    rotated = jnp.sum(gathered[...], axis=0)
    rotated = jnp.concatenate([rotated, pltpu.roll(rotated, 64, 1)], axis=0)
    for half in (0, 1):
        wait_bytes(last_gathered.at[pl.ds(0, 16)], q_recv.at[half])
    lane = lax.broadcasted_iota(jnp.int32, (8, 128), 1)
    sums = [jnp.sum(last_gathered[half * 16 : half * 16 + 16], axis=0) for half in (0, 1)]
    rows = []
    for b in range(4):
        low, high = (pltpu.roll(sums[half], (128 + 32 * (half - b)) % 128, 1) for half in (0, 1))
        rows.append(jnp.where(lane < 32, low, high))
    rotated = (rotated + jnp.concatenate(rows, axis=0))[:, :64]
    moment = 0.95 * sm_ref[...] + 0.05 * rotated * rotated
    mom_ref[...] = moment
    step_ref[...] = rotated / (jnp.sqrt(moment) + 1e-08)

    for copy in started:
        copy.wait_send()
    for s, u in scattered:
        copy, _, _, ahead = hidden_copy(s, u)

        @pl.when(ahead != 0)
        def _():
            copy.wait_send()

    for q in range(4):

        @pl.when((distance(x_first + q) < DIRECT) & (y_lo != q // 2))
        def _():
            to_pair(q).wait_send()

    wait_bytes(gathered.at[pl.ds(0, 15)], w_send)
    swap_rot.wait_send()
    swap_last.wait_send()

    @pl.when(own_last)
    def _():
        wait_bytes(last_gathered.at[pl.ds(0, 31)], q_send)

    @pl.when(jnp.logical_not(own_last))
    def _():
        wait_bytes(last_gathered, q_send)


def shards(gradient, right_panel, left_panel, second_moment):
    panel_t = right_panel.T.reshape(2, 8, FFL)
    anywhere = pl.BlockSpec(memory_space=pl.ANY)
    vmem = pl.BlockSpec(memory_space=pltpu.VMEM)
    dma = pltpu.SemaphoreType.DMA
    return pl.pallas_call(
        kernel,
        out_shape=[jax.ShapeDtypeStruct(second_moment.shape, F32)] * 2,
        in_specs=[anywhere, anywhere, anywhere, vmem],
        out_specs=[vmem, vmem],
        scratch_shapes=[
            pltpu.VMEM((64, 8, FFL), F32),
            pltpu.VMEM((ROWS, FFL), BF16),
            pltpu.VMEM((ROWS, LEFT), BF16),
            pltpu.VMEM((LEFT, ROWS), BF16),
            pltpu.VMEM((256, ROWS), F32),
            pltpu.VMEM((512, ROWS), F32),
            pltpu.VMEM((8, 2, 32, ROWS), F32),
            pltpu.VMEM((4, 4, 32, ROWS), F32),
            pltpu.VMEM((2, 32, ROWS), F32),
            pltpu.VMEM((2, 32, ROWS), F32),
            pltpu.VMEM((2, 32, ROWS), F32),
            pltpu.VMEM((128, ROWS), BF16),
            pltpu.VMEM((2, 16, 16, 128), F32),
            pltpu.VMEM((16, 16, 128), F32),
            pltpu.VMEM((16, 16, 128), F32),
            pltpu.VMEM((2, 16, 2, 8, 128), F32),
            pltpu.VMEM((16, 2, 8, 128), F32),
            pltpu.VMEM((32, 8, 128), F32),
            dma, dma, dma, dma((24,)), dma((24,)), dma((10,)), dma((10,)), dma((18,)), dma((7,)),
            dma((16,)), dma((2,)), dma((2,)), dma((2,)), dma((4,)), dma, dma,
            dma((2,)), dma((2,)), dma, dma((2,)),
        ],
        compiler_params=pltpu.CompilerParams(
            collective_id=0, has_side_effects=True, vmem_limit_bytes=60 * 2**20
        ),
    )(panel_t, gradient, left_panel, second_moment)


def solution(mesh):
    placed = (P("wide", "narrow"), P("narrow", "wide"), P("wide", None), P("wide", "narrow"))
    return jax.shard_map(
        shards,
        mesh=mesh,
        in_specs=placed,
        out_specs=(P("wide", "narrow"), P("wide", "narrow")),
        check_vma=False,
    )
```

```python
import functools

import jax
import jax.numpy as jnp
from jax import lax
from jax.experimental import pallas as pl
from jax.experimental.pallas import tpu as pltpu
from jax.sharding import PartitionSpec as P

MESH = pl.DeviceIdType.MESH
NT = (((1,), (1,)), ((), ()))
F32, BF16 = jnp.float32, jnp.bfloat16

FFL = 6656
ROWS = 512
LEFT = 1024
TILE = 128
SPLIT = 24 * TILE
DIRECT = 3
A, B, A2 = 0, 1, 2
HALF_A = 12 * TILE
HALF_B = 14 * TILE


def lanes(s, way, kind):
    if kind == B:
        if s < 4:
            return SPLIT, FFL - SPLIT
        return (SPLIT, HALF_B) if way == 0 else (SPLIT + HALF_B, FFL - SPLIT - HALF_B)
    if s < 4:
        return 0, SPLIT
    return (0, HALF_A) if way == 0 else (HALF_A, SPLIT - HALF_A)


def unit(s, way, other):
    if s == 0:
        return other
    if s == 4:
        return 14 + other
    return 2 + (s - 1) * 4 + other * 2 + way


def kernel(
    rt_ref, g_ref, l_ref, out_ref,
    panel, grad, left, left_t, acc, hidden, parts, x_parts, y_out, y_in, mine, stack,
    rot, rot_in, gathered, last, last_in, last_gathered,
    own_sem, g_sem, l_sem, z_send, z_recv, y_send, y_recv, s_send, s_recv,
    n_send, n_recv, p_send, p_recv, x_recv, w_send, w_recv,
    e_send, e_recv, q_send, q_recv,
):
    w, n = lax.axis_index("wide"), lax.axis_index("narrow")
    yh, z, core = w // 16, lax.rem(w // 2, 8), lax.rem(w, 2)

    def at(y_hi, zz, cc):
        return (y_hi * 16 + lax.rem(zz + 16, 8) * 2 + cc, n)

    ring = (at(yh, z + 1, core), at(yh, z - 1, core))
    across = at(1 - yh, z, core)
    sibling = at(yh, z, 1 - core)

    own = pltpu.make_async_copy(rt_ref, panel.at[pl.ds(core * 2, 2)], own_sem)
    own.start()
    load_g = pltpu.make_async_copy(g_ref, grad, g_sem)
    load_g.start()
    load_l = pltpu.make_async_copy(l_ref, left, l_sem)
    load_l.start()

    barrier = pltpu.get_barrier_semaphore()
    greet = [*ring, across, sibling]
    greet += [(w, lax.rem(n + i, 8)) for i in range(1, 8)]
    for device in greet:
        pl.semaphore_signal(barrier, inc=1, device_id=device, device_id_type=MESH)
    own.wait()
    pl.semaphore_wait(barrier, len(greet))

    def block(u, first, size):
        return panel.at[pl.ds(u * 4 + core * 2, 2), :, pl.ds(first, size)]

    def remote(src, dst, send, recv, device):
        return pltpu.make_async_remote_copy(
            src_ref=src, dst_ref=dst, send_sem=send, recv_sem=recv, device_id=device, device_id_type=MESH
        )

    started = []

    def start(copy):
        copy.start()
        started.append(copy)

    def along_z(s, way, kind):
        first, size = lanes(s, way, kind)
        other = int(kind == A2)
        which = way * 12 + (s - 1) * 3 + kind
        return remote(
            block(unit(s - 1, way, other), first, size),
            block(unit(s, way, other), first, size),
            z_send.at[which], z_recv.at[which], ring[way],
        )

    def along_y(s, way, kind):
        first, size = lanes(s, way, kind)
        which = int(kind == B) if s == 0 else 2 + (s - 1) * 2 + way
        return remote(
            block(unit(s, way, 0), first, size), block(unit(s, way, 1), first, size),
            y_send.at[which], y_recv.at[which], across,
        )

    def to_sibling(u, group, first=0, size=FFL, slot=0):
        part = block(u, first, size)
        start(remote(part, part, s_send.at[u + 2 * slot], s_recv.at[group], sibling))

    def wait_bytes(ref, sem):
        pltpu.make_async_copy(ref, ref, sem).wait()

    def multiply(first_block, blocks, first, size, step, fresh):
        rows = blocks * 8

        def body(i, carry):
            cols = pl.ds(pl.multiple_of(first + i * step, TILE), step)
            value = panel[pl.ds(first_block, blocks), :, cols].reshape(rows, step)
            high = value.astype(BF16)
            low = (value - high.astype(F32)).astype(BF16)
            both = jnp.concatenate([high, low], axis=0)
            acc[: 2 * rows] += lax.dot_general(both, grad[:, cols], NT, preferred_element_type=F32)
            return carry

        if fresh:
            acc[: 2 * rows] = jnp.zeros((2 * rows, ROWS), F32)
        lax.fori_loop(0, size // step, body, 0)

    def hidden_copy(s, u):
        way, other = (u % 2, (u - 2) % 4 // 2) if 0 < s < 4 else (0, u % 2)
        zz = lax.rem(z + (s if way == 1 else -s) + 8, 8)
        there = yh if other == 0 else 1 - yh
        source = hidden.at[pl.ds(u * 32, 32)]
        if s >= DIRECT:
            keeper = there * 4 + zz // 2
            ahead = lax.rem(keeper - n + 8, 8)
            half = lax.rem(zz, 2)
            return (
                remote(source, parts.at[7 - ahead, half], n_send.at[u], n_recv.at[half], (w, keeper)),
                source, parts.at[7, half], ahead,
            )
        keeper = there * 2 + zz // 4
        ahead = lax.rem(keeper - n // 2 + 4, 4)
        quarter = lax.rem(zz, 4)
        device = (w, keeper * 2 + lax.rem(n, 2))
        return (
            remote(source, x_parts.at[3 - ahead, quarter], n_send.at[u], x_recv.at[quarter], device),
            source, x_parts.at[3, quarter], ahead,
        )

    scattered = []

    def scatter(s, first_unit, units):
        rows = units * 32
        hidden[first_unit * 32 : first_unit * 32 + rows] = acc[:rows] + acc[rows : 2 * rows]
        for u in range(first_unit, first_unit + units):
            copy, source, here, ahead = hidden_copy(s, u)
            scattered.append((s, u))

            @pl.when(ahead == 0)
            def _():
                here[...] = source[...]

            @pl.when(ahead != 0)
            def _():
                copy.start()

    def distance(a):
        there = lax.rem(z - a + 8, 8)
        return jnp.minimum(there, lax.rem(8 - there, 8))

    x_first = 4 * lax.rem(n // 2, 2)
    y_lo = lax.rem(n, 2)

    def to_pair(q):
        return remote(y_out.at[q % 2], y_in.at[q % 2], p_send.at[q % 2], p_recv.at[q % 2], (w, n + 1 - 2 * y_lo))

    def reduce_x(s):
        for q in range(4):

            @pl.when(distance(x_first + q) == s)
            def _():
                wait_bytes(x_parts.at[pl.ds(0, 3), q], x_recv.at[q])
                total = x_parts[0, q] + x_parts[1, q] + x_parts[2, q] + x_parts[3, q]

                @pl.when(y_lo == q // 2)
                def _():
                    mine[q % 2] = total

                @pl.when(y_lo != q // 2)
                def _():
                    y_out[q % 2] = total
                    to_pair(q).start()

    first_z = 2 * lax.rem(n, 4)

    spot = w // 2

    def fill_stack(total):
        high = total.astype(BF16)
        stack[:64] = high
        stack[64:] = (total - high.astype(F32)).astype(BF16)

    def rotated_rows(i):
        cols = pl.ds(pl.multiple_of(i * 256, 256), 256)
        out = lax.dot_general(left_t[cols, :], stack[...], NT, preferred_element_type=F32)
        return out + pltpu.roll(out, 64, 1)

    swap_rot = remote(rot.at[1 - core], rot_in, e_send.at[0], e_recv.at[0], sibling)
    swap_last = remote(last.at[1 - core], last_in, e_send.at[1], e_recv.at[1], sibling)

    def rotate_start():
        for half in (0, 1):
            d = distance(first_z + half)

            @pl.when(d == 4)
            def _():
                mine[half] = jnp.zeros((32, ROWS), F32)

            @pl.when(d == DIRECT)
            def _():
                wait_bytes(parts.at[pl.ds(0, 7), half], n_recv.at[half])
                total = parts[0, half]
                for i in range(1, 8):
                    total = total + parts[i, half]
                mine[half] = total

            @pl.when(d < DIRECT)
            def _():
                wait_bytes(y_in.at[half], p_recv.at[half])
                mine[half] += y_in[half]

        fill_stack(mine[...].reshape(64, ROWS))

        def body(i, carry):
            out = rotated_rows(i).reshape(4, 2, 2, 16, 128)
            lane = lax.broadcasted_iota(jnp.int32, (4, 16, 128), 2)
            for c in (0, 1):
                rot[c, pl.ds(i * 4, 4)] = jnp.where(lane < 64, out[:, c, 0], out[:, c, 1])
            return carry

        lax.fori_loop(0, 4, body, 0)
        swap_rot.start()

    def rotate_finish():
        swap_rot.wait_recv()

        def add(k, carry):
            rot[core, k] += rot_in[k]
            return carry

        lax.fori_loop(0, 16, add, 0)

        def send(i, carry):
            k = lax.rem(spot + i, 16)
            remote(rot.at[core, k], gathered.at[i - 1], w_send, w_recv, (k * 2 + core, n)).start()
            return carry

        lax.fori_loop(1, 16, send, 0)
        gathered[15] = rot[core, spot]

    def last_start():
        fill_stack(acc[:64] + acc[64:128])

        def body(i, carry):
            out = rotated_rows(i)
            turned = pltpu.roll(out, 32, 1).reshape(4, 2, 4, 8, 128)
            out = out.reshape(4, 2, 4, 8, 128)
            which = lax.broadcasted_iota(jnp.int32, (4, 8, 128), 2) // 32
            for c in (0, 1):
                for other in (0, 1):
                    even, odd = (out, turned) if other == 0 else (turned, out)
                    value = jnp.where(which == 0, even[:, c, 0], odd[:, c, 1])
                    value = jnp.where(which == 2, even[:, c, 2], value)
                    last[c, pl.ds(i * 4, 4), other] = jnp.where(which == 3, odd[:, c, 3], value)
            return carry

        lax.fori_loop(0, 4, body, 0)
        swap_last.start()

    far_chip = lax.rem(z + 4, 8)
    own_last = lax.rem(n, 4) == far_chip // 2

    def last_finish():
        swap_last.wait_recv()

        def add(k, carry):
            last[core, k] += last_in[k]
            return carry

        lax.fori_loop(0, 16, add, 0)
        half = lax.rem(z, 2)
        slot = half * 16 + yh * 8 + n

        def send(i, carry):
            k = lax.rem(spot + i, 16)
            for other in (0, 1):
                keeper = (yh if other == 0 else 1 - yh) * 4 + far_chip // 2
                here = (k == spot) & (keeper == n)
                source, target = last.at[core, k, other], last_gathered.at[slot]

                @pl.when(here)
                def _():
                    pltpu.make_async_copy(source, target, q_recv.at[half]).start()

                @pl.when(jnp.logical_not(here))
                def _():
                    remote(source, target, q_send, q_recv.at[half], (k * 2 + core, keeper)).start()

            return carry

        lax.fori_loop(0, 16, send, 0)

    last_step = jnp.maximum(distance(first_z), distance(first_z + 1))

    start(along_y(0, 0, A))
    for way in (0, 1):
        start(along_z(1, way, B))
    to_sibling(0, 0)
    for way in (0, 1):
        start(along_z(1, way, A))
    start(along_y(0, 0, B))

    load_l.wait()

    def turn(i, carry):
        cols = pl.ds(pl.multiple_of(i * 256, 256), 256)
        left_t[cols, :] = left[:, cols].T
        return carry

    lax.fori_loop(0, 4, turn, 0)

    along_y(0, 0, A).wait_recv()
    for way in (0, 1):
        start(along_z(1, way, A2))

    def forward_b(s):
        for way in (0, 1):
            along_z(s, way, B).wait_recv()
            if s < 4:
                start(along_z(s + 1, way, B))
            start(along_y(s, way, B))

    def forward_a(s):
        for way in (0, 1):
            along_z(s, way, A).wait_recv()
            if s < 4:
                start(along_z(s + 1, way, A))
                to_sibling(unit(s, way, 0), s)

    def forward_a2(s):
        for way in (0, 1):
            along_z(s, way, A2).wait_recv()
            if s < 4:
                start(along_z(s + 1, way, A2))

    def settle_y(s):
        for way in (0, 1):
            along_y(s, way, B).wait_recv()
            if s < 4:
                to_sibling(unit(s, way, 1), 6 if s == 3 else s)

    def compute(s):
        wait_bytes(panel.at[pl.ds(0, 8)], s_recv.at[s])
        multiply(unit(s, 0, 0) * 4, 16, 0, FFL, 1664, True)
        scatter(s, unit(s, 0, 0), 4)

    forward_b(1)
    forward_a(1)
    along_y(0, 0, B).wait_recv()
    to_sibling(1, 0)
    load_g.wait()
    wait_bytes(panel.at[pl.ds(0, 4)], s_recv.at[0])
    multiply(0, 8, 0, FFL, 1664, True)
    scatter(0, 0, 2)
    forward_b(2)
    forward_a2(1)
    settle_y(1)
    forward_a(2)
    compute(1)
    reduce_x(0)
    forward_b(3)
    forward_a2(2)
    settle_y(2)
    compute(2)
    reduce_x(1)
    forward_a(3)
    forward_b(4)
    to_sibling(14, 4, SPLIT, FFL - SPLIT, 0)
    wait_bytes(panel.at[pl.ds(0, 4)], s_recv.at[3])
    multiply(unit(3, 0, 0) * 4, 8, 0, FFL, 1664, True)
    scatter(3, unit(3, 0, 0), 2)
    reduce_x(2)
    forward_a2(3)
    settle_y(3)
    wait_bytes(panel.at[pl.ds(0, 4)], s_recv.at[6])
    multiply(unit(3, 0, 1) * 4, 8, 0, FFL, 1664, True)
    scatter(3, unit(3, 0, 1), 2)
    forward_a(4)
    to_sibling(14, 5, 0, SPLIT, 1)

    @pl.when(last_step <= 2)
    def _():
        rotate_start()

    forward_a2(4)
    to_sibling(15, 5, 0, SPLIT, 1)

    @pl.when(last_step <= 2)
    def _():
        rotate_finish()

    settle_y(4)
    to_sibling(15, 4, SPLIT, FFL - SPLIT, 0)
    wait_bytes(panel.at[pl.ds(0, 4), :, pl.ds(0, SPLIT)], s_recv.at[5])
    multiply(56, 8, 0, SPLIT, SPLIT // 2, True)
    wait_bytes(panel.at[pl.ds(0, 4), :, pl.ds(SPLIT, FFL - SPLIT)], s_recv.at[4])
    multiply(56, 8, SPLIT, FFL - SPLIT, (FFL - SPLIT) // 2, False)
    last_start()

    last_finish()

    @pl.when(last_step > 2)
    def _():
        rotate_start()

    @pl.when(last_step > 2)
    def _():
        rotate_finish()

    for copy in started:
        copy.wait_send()
    for s, u in scattered:
        copy, _, _, ahead = hidden_copy(s, u)

        @pl.when(ahead != 0)
        def _():
            copy.wait_send()

    for q in range(4):

        @pl.when((distance(x_first + q) < DIRECT) & (y_lo != q // 2))
        def _():
            to_pair(q).wait_send()

    wait_bytes(gathered.at[pl.ds(0, 15)], w_recv)
    rotated = jnp.sum(gathered[...], axis=0)
    rotated = jnp.concatenate([rotated, pltpu.roll(rotated, 64, 1)], axis=0)
    for half in (0, 1):
        wait_bytes(last_gathered.at[pl.ds(0, 16)], q_recv.at[half])
    lane = lax.broadcasted_iota(jnp.int32, (8, 128), 1)
    sums = [jnp.sum(last_gathered[half * 16 : half * 16 + 16], axis=0) for half in (0, 1)]
    rows = []
    for b in range(4):
        low, high = (pltpu.roll(sums[half], (128 + 32 * (half - b)) % 128, 1) for half in (0, 1))
        rows.append(jnp.where(lane < 32, low, high))
    rotated = (rotated + jnp.concatenate(rows, axis=0))[:, :64]
    out_ref[...] = rotated

    wait_bytes(gathered.at[pl.ds(0, 15)], w_send)
    swap_rot.wait_send()
    swap_last.wait_send()

    @pl.when(own_last)
    def _():
        wait_bytes(last_gathered.at[pl.ds(0, 31)], q_send)

    @pl.when(jnp.logical_not(own_last))
    def _():
        wait_bytes(last_gathered, q_send)


def shards(gradient, right_panel, left_panel, second_moment):
    panel_t = right_panel.T.reshape(2, 8, FFL)
    anywhere = pl.BlockSpec(memory_space=pl.ANY)
    dma = pltpu.SemaphoreType.DMA
    rotated = pl.pallas_call(
        kernel,
        out_shape=jax.ShapeDtypeStruct(second_moment.shape, F32),
        in_specs=[anywhere] * 3,
        out_specs=pl.BlockSpec(memory_space=pltpu.VMEM),
        scratch_shapes=[
            pltpu.VMEM((64, 8, FFL), F32),
            pltpu.VMEM((ROWS, FFL), BF16),
            pltpu.VMEM((ROWS, LEFT), BF16),
            pltpu.VMEM((LEFT, ROWS), BF16),
            pltpu.VMEM((256, ROWS), F32),
            pltpu.VMEM((512, ROWS), F32),
            pltpu.VMEM((8, 2, 32, ROWS), F32),
            pltpu.VMEM((4, 4, 32, ROWS), F32),
            pltpu.VMEM((2, 32, ROWS), F32),
            pltpu.VMEM((2, 32, ROWS), F32),
            pltpu.VMEM((2, 32, ROWS), F32),
            pltpu.VMEM((128, ROWS), BF16),
            pltpu.VMEM((2, 16, 16, 128), F32),
            pltpu.VMEM((16, 16, 128), F32),
            pltpu.VMEM((16, 16, 128), F32),
            pltpu.VMEM((2, 16, 2, 8, 128), F32),
            pltpu.VMEM((16, 2, 8, 128), F32),
            pltpu.VMEM((32, 8, 128), F32),
            dma, dma, dma, dma((24,)), dma((24,)), dma((10,)), dma((10,)), dma((18,)), dma((7,)),
            dma((16,)), dma((2,)), dma((2,)), dma((2,)), dma((4,)), dma, dma,
            dma((2,)), dma((2,)), dma, dma((2,)),
        ],
        compiler_params=pltpu.CompilerParams(
            collective_id=0, has_side_effects=True, vmem_limit_bytes=60 * 2**20
        ),
    )(panel_t, gradient, left_panel)
    moment_new = 0.95 * second_moment + 0.05 * rotated * rotated
    return moment_new, rotated / (jnp.sqrt(moment_new) + 1e-08)


def solution(mesh):
    placed = (P("wide", "narrow"), P("narrow", "wide"), P("wide", None), P("wide", "narrow"))
    return jax.shard_map(
        shards,
        mesh=mesh,
        in_specs=placed,
        out_specs=(P("wide", "narrow"), P("wide", "narrow")),
        check_vma=False,
    )
```

```python
import functools

import jax
import jax.numpy as jnp
from jax import lax
from jax.experimental import pallas as pl
from jax.experimental.pallas import tpu as pltpu
from jax.sharding import PartitionSpec as P

MESH = pl.DeviceIdType.MESH
NT = (((1,), (1,)), ((), ()))
F32, BF16 = jnp.float32, jnp.bfloat16

FFL = 6656
ROWS = 512
LEFT = 1024
TILE = 128
SPLIT = 24 * TILE
DIRECT = 3
A, B, A2 = 0, 1, 2
HALF_A = 12 * TILE
HALF_B = 14 * TILE


def lanes(s, way, kind):
    if kind == B:
        if s < 4:
            return SPLIT, FFL - SPLIT
        return (SPLIT, HALF_B) if way == 0 else (SPLIT + HALF_B, FFL - SPLIT - HALF_B)
    if s < 4:
        return 0, SPLIT
    return (0, HALF_A) if way == 0 else (HALF_A, SPLIT - HALF_A)


def unit(s, way, other):
    if s == 0:
        return other
    if s == 4:
        return 14 + other
    return 2 + (s - 1) * 4 + other * 2 + way


def kernel(
    rt_ref, g_ref, l_ref, out_ref,
    panel, grad, left, left_t, acc, hidden, parts, x_parts, y_out, y_in, mine, stack,
    rot, rot_in, gathered, last, last_in, last_gathered,
    own_sem, g_sem, l_sem, z_send, z_recv, y_send, y_recv, s_send, s_recv,
    n_send, n_recv, p_send, p_recv, x_recv, w_send, w_recv,
    e_send, e_recv, q_send, q_recv,
):
    w, n = lax.axis_index("wide"), lax.axis_index("narrow")
    yh, z, core = w // 16, lax.rem(w // 2, 8), lax.rem(w, 2)

    def at(y_hi, zz, cc):
        return (y_hi * 16 + lax.rem(zz + 16, 8) * 2 + cc, n)

    ring = (at(yh, z + 1, core), at(yh, z - 1, core))
    across = at(1 - yh, z, core)
    sibling = at(yh, z, 1 - core)

    own = pltpu.make_async_copy(rt_ref, panel.at[pl.ds(core * 2, 2)], own_sem)
    own.start()
    load_g = pltpu.make_async_copy(g_ref, grad, g_sem)
    load_g.start()
    load_l = pltpu.make_async_copy(l_ref, left, l_sem)
    load_l.start()

    barrier = pltpu.get_barrier_semaphore()
    greet = [*ring, across, sibling]
    greet += [(w, lax.rem(n + i, 8)) for i in range(1, 8)]
    for device in greet:
        pl.semaphore_signal(barrier, inc=1, device_id=device, device_id_type=MESH)
    own.wait()
    pl.semaphore_wait(barrier, len(greet))

    def block(u, first, size):
        return panel.at[pl.ds(u * 4 + core * 2, 2), :, pl.ds(first, size)]

    def remote(src, dst, send, recv, device):
        return pltpu.make_async_remote_copy(
            src_ref=src, dst_ref=dst, send_sem=send, recv_sem=recv, device_id=device, device_id_type=MESH
        )

    started = []

    def start(copy):
        copy.start()
        started.append(copy)

    def along_z(s, way, kind):
        first, size = lanes(s, way, kind)
        other = int(kind == A2)
        which = way * 12 + (s - 1) * 3 + kind
        return remote(
            block(unit(s - 1, way, other), first, size),
            block(unit(s, way, other), first, size),
            z_send.at[which], z_recv.at[which], ring[way],
        )

    def along_y(s, way, kind):
        first, size = lanes(s, way, kind)
        which = int(kind == B) if s == 0 else 2 + (s - 1) * 2 + way
        return remote(
            block(unit(s, way, 0), first, size), block(unit(s, way, 1), first, size),
            y_send.at[which], y_recv.at[which], across,
        )

    def to_sibling(u, group, first=0, size=FFL, slot=0):
        part = block(u, first, size)
        start(remote(part, part, s_send.at[u + 2 * slot], s_recv.at[group], sibling))

    def wait_bytes(ref, sem):
        pltpu.make_async_copy(ref, ref, sem).wait()

    def multiply(first_block, blocks, first, size, step, fresh):
        rows = blocks * 8

        def body(i, carry):
            cols = pl.ds(pl.multiple_of(first + i * step, TILE), step)
            value = panel[pl.ds(first_block, blocks), :, cols].reshape(rows, step)
            high = value.astype(BF16)
            low = (value - high.astype(F32)).astype(BF16)
            both = jnp.concatenate([high, low], axis=0)
            acc[: 2 * rows] += lax.dot_general(both, grad[:, cols], NT, preferred_element_type=F32)
            return carry

        if fresh:
            acc[: 2 * rows] = jnp.zeros((2 * rows, ROWS), F32)
        lax.fori_loop(0, size // step, body, 0)

    def hidden_copy(s, u):
        way, other = (u % 2, (u - 2) % 4 // 2) if 0 < s < 4 else (0, u % 2)
        zz = lax.rem(z + (s if way == 1 else -s) + 8, 8)
        there = yh if other == 0 else 1 - yh
        source = hidden.at[pl.ds(u * 32, 32)]
        if s == DIRECT and other == 1:
            keeper = there * 4 + zz // 2
            ahead = lax.rem(keeper - n + 8, 8)
            half = lax.rem(zz, 2)
            return (
                remote(source, parts.at[7 - ahead, half], n_send.at[u], n_recv.at[half], (w, keeper)),
                source, parts.at[7, half], ahead,
            )
        keeper = there * 2 + zz // 4
        ahead = lax.rem(keeper - n // 2 + 4, 4)
        quarter = lax.rem(zz, 4)
        device = (w, keeper * 2 + lax.rem(n, 2))
        return (
            remote(source, x_parts.at[3 - ahead, quarter], n_send.at[u], x_recv.at[quarter], device),
            source, x_parts.at[3, quarter], ahead,
        )

    scattered = []

    def scatter(s, first_unit, units):
        rows = units * 32
        hidden[first_unit * 32 : first_unit * 32 + rows] = acc[:rows] + acc[rows : 2 * rows]
        for u in range(first_unit, first_unit + units):
            copy, source, here, ahead = hidden_copy(s, u)
            scattered.append((s, u))

            @pl.when(ahead == 0)
            def _():
                here[...] = source[...]

            @pl.when(ahead != 0)
            def _():
                copy.start()

    def distance(a):
        there = lax.rem(z - a + 8, 8)
        return jnp.minimum(there, lax.rem(8 - there, 8))

    first_z = 2 * lax.rem(n, 4)
    same_line = n // 4 == yh

    def by_x(d):
        return (d < DIRECT) | ((d == DIRECT) & same_line)

    x_first = 4 * lax.rem(n // 2, 2)
    y_lo = lax.rem(n, 2)

    def to_pair(q):
        return remote(y_out.at[q % 2], y_in.at[q % 2], p_send.at[q % 2], p_recv.at[q % 2], (w, n + 1 - 2 * y_lo))

    def reduce_x(s):
        for q in range(4):

            @pl.when((distance(x_first + q) == s) & ((s < DIRECT) | same_line))
            def _():
                wait_bytes(x_parts.at[pl.ds(0, 3), q], x_recv.at[q])
                total = x_parts[0, q] + x_parts[1, q] + x_parts[2, q] + x_parts[3, q]

                @pl.when(y_lo == q // 2)
                def _():
                    mine[q % 2] = total

                @pl.when(y_lo != q // 2)
                def _():
                    y_out[q % 2] = total
                    to_pair(q).start()


    spot = w // 2

    def fill_stack(total):
        high = total.astype(BF16)
        stack[:64] = high
        stack[64:] = (total - high.astype(F32)).astype(BF16)

    def rotated_rows(i):
        cols = pl.ds(pl.multiple_of(i * 256, 256), 256)
        out = lax.dot_general(left_t[cols, :], stack[...], NT, preferred_element_type=F32)
        return out + pltpu.roll(out, 64, 1)

    swap_rot = remote(rot.at[1 - core], rot_in, e_send.at[0], e_recv.at[0], sibling)
    swap_last = remote(last.at[1 - core], last_in, e_send.at[1], e_recv.at[1], sibling)

    def rotate_start():
        for half in (0, 1):
            d = distance(first_z + half)

            @pl.when(d == 4)
            def _():
                mine[half] = jnp.zeros((32, ROWS), F32)

            @pl.when((d == DIRECT) & jnp.logical_not(same_line))
            def _():
                wait_bytes(parts.at[pl.ds(0, 7), half], n_recv.at[half])
                total = parts[0, half]
                for i in range(1, 8):
                    total = total + parts[i, half]
                mine[half] = total

            @pl.when(by_x(d))
            def _():
                wait_bytes(y_in.at[half], p_recv.at[half])
                mine[half] += y_in[half]

        fill_stack(mine[...].reshape(64, ROWS))

        def body(i, carry):
            out = rotated_rows(i).reshape(4, 2, 2, 16, 128)
            lane = lax.broadcasted_iota(jnp.int32, (4, 16, 128), 2)
            for c in (0, 1):
                rot[c, pl.ds(i * 4, 4)] = jnp.where(lane < 64, out[:, c, 0], out[:, c, 1])
            return carry

        lax.fori_loop(0, 4, body, 0)
        swap_rot.start()

    def rotate_finish():
        swap_rot.wait_recv()

        def add(k, carry):
            rot[core, k] += rot_in[k]
            return carry

        lax.fori_loop(0, 16, add, 0)

        def send(i, carry):
            k = lax.rem(spot + i, 16)
            remote(rot.at[core, k], gathered.at[i - 1], w_send, w_recv, (k * 2 + core, n)).start()
            return carry

        lax.fori_loop(1, 16, send, 0)
        gathered[15] = rot[core, spot]

    def last_start():
        fill_stack(acc[:64] + acc[64:128])

        def body(i, carry):
            out = rotated_rows(i)
            turned = pltpu.roll(out, 32, 1).reshape(4, 2, 4, 8, 128)
            out = out.reshape(4, 2, 4, 8, 128)
            which = lax.broadcasted_iota(jnp.int32, (4, 8, 128), 2) // 32
            for c in (0, 1):
                for other in (0, 1):
                    even, odd = (out, turned) if other == 0 else (turned, out)
                    value = jnp.where(which == 0, even[:, c, 0], odd[:, c, 1])
                    value = jnp.where(which == 2, even[:, c, 2], value)
                    last[c, pl.ds(i * 4, 4), other] = jnp.where(which == 3, odd[:, c, 3], value)
            return carry

        lax.fori_loop(0, 4, body, 0)
        swap_last.start()

    far_chip = lax.rem(z + 4, 8)
    own_last = lax.rem(n, 4) == far_chip // 2

    def last_finish():
        swap_last.wait_recv()

        def add(k, carry):
            last[core, k] += last_in[k]
            return carry

        lax.fori_loop(0, 16, add, 0)
        half = lax.rem(z, 2)
        slot = half * 16 + yh * 8 + n

        def send(i, carry):
            k = lax.rem(spot + i, 16)
            for other in (0, 1):
                keeper = (yh if other == 0 else 1 - yh) * 4 + far_chip // 2
                here = (k == spot) & (keeper == n)
                source, target = last.at[core, k, other], last_gathered.at[slot]

                @pl.when(here)
                def _():
                    pltpu.make_async_copy(source, target, q_recv.at[half]).start()

                @pl.when(jnp.logical_not(here))
                def _():
                    remote(source, target, q_send, q_recv.at[half], (k * 2 + core, keeper)).start()

            return carry

        lax.fori_loop(0, 16, send, 0)

    last_step = jnp.maximum(distance(first_z), distance(first_z + 1))

    start(along_y(0, 0, A))
    for way in (0, 1):
        start(along_z(1, way, B))
    to_sibling(0, 0)
    for way in (0, 1):
        start(along_z(1, way, A))
    start(along_y(0, 0, B))

    load_l.wait()

    def turn(i, carry):
        cols = pl.ds(pl.multiple_of(i * 256, 256), 256)
        left_t[cols, :] = left[:, cols].T
        return carry

    lax.fori_loop(0, 4, turn, 0)

    along_y(0, 0, A).wait_recv()
    for way in (0, 1):
        start(along_z(1, way, A2))

    def forward_b(s):
        for way in (0, 1):
            along_z(s, way, B).wait_recv()
            if s < 4:
                start(along_z(s + 1, way, B))
            start(along_y(s, way, B))

    def forward_a(s):
        for way in (0, 1):
            along_z(s, way, A).wait_recv()
            if s < 4:
                start(along_z(s + 1, way, A))
                to_sibling(unit(s, way, 0), s)

    def forward_a2(s):
        for way in (0, 1):
            along_z(s, way, A2).wait_recv()
            if s < 4:
                start(along_z(s + 1, way, A2))

    def settle_y(s):
        for way in (0, 1):
            along_y(s, way, B).wait_recv()
            if s < 4:
                to_sibling(unit(s, way, 1), 6 if s == 3 else s)

    def compute(s):
        wait_bytes(panel.at[pl.ds(0, 8)], s_recv.at[s])
        multiply(unit(s, 0, 0) * 4, 16, 0, FFL, 1664, True)
        scatter(s, unit(s, 0, 0), 4)

    forward_b(1)
    forward_a(1)
    along_y(0, 0, B).wait_recv()
    to_sibling(1, 0)
    load_g.wait()
    wait_bytes(panel.at[pl.ds(0, 4)], s_recv.at[0])
    multiply(0, 8, 0, FFL, 1664, True)
    scatter(0, 0, 2)
    forward_b(2)
    forward_a2(1)
    settle_y(1)
    forward_a(2)
    compute(1)
    reduce_x(0)
    forward_b(3)
    forward_a2(2)
    settle_y(2)
    compute(2)
    reduce_x(1)
    forward_a(3)
    forward_b(4)
    to_sibling(14, 4, SPLIT, FFL - SPLIT, 0)
    wait_bytes(panel.at[pl.ds(0, 4)], s_recv.at[3])
    multiply(unit(3, 0, 0) * 4, 8, 0, FFL, 1664, True)
    scatter(3, unit(3, 0, 0), 2)
    reduce_x(2)
    forward_a2(3)
    settle_y(3)
    wait_bytes(panel.at[pl.ds(0, 4)], s_recv.at[6])
    multiply(unit(3, 0, 1) * 4, 8, 0, FFL, 1664, True)
    scatter(3, unit(3, 0, 1), 2)
    reduce_x(3)
    forward_a(4)
    to_sibling(14, 5, 0, SPLIT, 1)

    @pl.when(last_step <= 2)
    def _():
        rotate_start()

    forward_a2(4)
    to_sibling(15, 5, 0, SPLIT, 1)

    @pl.when(last_step <= 2)
    def _():
        rotate_finish()

    settle_y(4)
    to_sibling(15, 4, SPLIT, FFL - SPLIT, 0)
    wait_bytes(panel.at[pl.ds(0, 4), :, pl.ds(0, SPLIT)], s_recv.at[5])
    multiply(56, 8, 0, SPLIT, SPLIT // 2, True)
    wait_bytes(panel.at[pl.ds(0, 4), :, pl.ds(SPLIT, FFL - SPLIT)], s_recv.at[4])
    multiply(56, 8, SPLIT, FFL - SPLIT, (FFL - SPLIT) // 2, False)
    last_start()

    last_finish()

    @pl.when(last_step > 2)
    def _():
        rotate_start()

    @pl.when(last_step > 2)
    def _():
        rotate_finish()

    for copy in started:
        copy.wait_send()
    for s, u in scattered:
        copy, _, _, ahead = hidden_copy(s, u)

        @pl.when(ahead != 0)
        def _():
            copy.wait_send()

    for q in range(4):

        @pl.when(by_x(distance(x_first + q)) & (y_lo != q // 2))
        def _():
            to_pair(q).wait_send()

    wait_bytes(gathered.at[pl.ds(0, 15)], w_recv)
    rotated = jnp.sum(gathered[...], axis=0)
    rotated = jnp.concatenate([rotated, pltpu.roll(rotated, 64, 1)], axis=0)
    for half in (0, 1):
        wait_bytes(last_gathered.at[pl.ds(0, 16)], q_recv.at[half])
    lane = lax.broadcasted_iota(jnp.int32, (8, 128), 1)
    sums = [jnp.sum(last_gathered[half * 16 : half * 16 + 16], axis=0) for half in (0, 1)]
    rows = []
    for b in range(4):
        low, high = (pltpu.roll(sums[half], (128 + 32 * (half - b)) % 128, 1) for half in (0, 1))
        rows.append(jnp.where(lane < 32, low, high))
    rotated = (rotated + jnp.concatenate(rows, axis=0))[:, :64]
    out_ref[...] = rotated

    wait_bytes(gathered.at[pl.ds(0, 15)], w_send)
    swap_rot.wait_send()
    swap_last.wait_send()

    @pl.when(own_last)
    def _():
        wait_bytes(last_gathered.at[pl.ds(0, 31)], q_send)

    @pl.when(jnp.logical_not(own_last))
    def _():
        wait_bytes(last_gathered, q_send)


def shards(gradient, right_panel, left_panel, second_moment):
    panel_t = right_panel.T.reshape(2, 8, FFL)
    anywhere = pl.BlockSpec(memory_space=pl.ANY)
    dma = pltpu.SemaphoreType.DMA
    rotated = pl.pallas_call(
        kernel,
        out_shape=jax.ShapeDtypeStruct(second_moment.shape, F32),
        in_specs=[anywhere] * 3,
        out_specs=pl.BlockSpec(memory_space=pltpu.VMEM),
        scratch_shapes=[
            pltpu.VMEM((64, 8, FFL), F32),
            pltpu.VMEM((ROWS, FFL), BF16),
            pltpu.VMEM((ROWS, LEFT), BF16),
            pltpu.VMEM((LEFT, ROWS), BF16),
            pltpu.VMEM((256, ROWS), F32),
            pltpu.VMEM((512, ROWS), F32),
            pltpu.VMEM((8, 2, 32, ROWS), F32),
            pltpu.VMEM((4, 4, 32, ROWS), F32),
            pltpu.VMEM((2, 32, ROWS), F32),
            pltpu.VMEM((2, 32, ROWS), F32),
            pltpu.VMEM((2, 32, ROWS), F32),
            pltpu.VMEM((128, ROWS), BF16),
            pltpu.VMEM((2, 16, 16, 128), F32),
            pltpu.VMEM((16, 16, 128), F32),
            pltpu.VMEM((16, 16, 128), F32),
            pltpu.VMEM((2, 16, 2, 8, 128), F32),
            pltpu.VMEM((16, 2, 8, 128), F32),
            pltpu.VMEM((32, 8, 128), F32),
            dma, dma, dma, dma((24,)), dma((24,)), dma((10,)), dma((10,)), dma((18,)), dma((7,)),
            dma((16,)), dma((2,)), dma((2,)), dma((2,)), dma((4,)), dma, dma,
            dma((2,)), dma((2,)), dma, dma((2,)),
        ],
        compiler_params=pltpu.CompilerParams(
            collective_id=0, has_side_effects=True, vmem_limit_bytes=60 * 2**20
        ),
    )(panel_t, gradient, left_panel)
    moment_new = 0.95 * second_moment + 0.05 * rotated * rotated
    return moment_new, rotated / (jnp.sqrt(moment_new) + 1e-08)


def solution(mesh):
    placed = (P("wide", "narrow"), P("narrow", "wide"), P("wide", None), P("wide", "narrow"))
    return jax.shard_map(
        shards,
        mesh=mesh,
        in_specs=placed,
        out_specs=(P("wide", "narrow"), P("wide", "narrow")),
        check_vma=False,
    )
```
